32 devices in a mesh: row: 4 (over x, core), col: 4 (over z), kern: 2 (over y).
Axes of the slice: x: 2, y: 2, z: 4, core: 2. Of those that a mesh axis runs over, the one named last changes fastest.
Arguments:
- mask_levels: int32 [128, 2048], P('row', 'col'), may hold values from 0 to 3
- level_offset: float32 [128, 2048], P('row', 'col'), may hold values from -6 to 6
- target_bits: int32 [128, 2048], P('row', 'col'), may hold values 0 or 1
- socs_kernels: bfloat16 [2, 24, 35, 35], P(None, 'kern'), may hold values from -0.067871094 to 0.067871094
- kernel_weights: float32 [24], P('kern'), may hold values from 0.1 to 1
Outputs:
- resist_image: float32 [128, 2048], P('row', 'col')
- mask_gradient: float32 [128, 2048], P('row', 'col')
The draws below stay inside these ranges and needn't reach their ends.
All inputs are finite; a program needn't handle non-finite values. No bound on the sum of `target_bits` on one device may be relied on, other than what follows from the above.
Results may differ from the reference program's by a relative error of at most 0.0039.
Values may be sent and summed in bfloat16 or wider, within the bound.
A program may use at most 64 MiB of HBM per device.

```python
import math
import jax
import jax.numpy as jnp
from jax import lax

K = 24
TAPS = 35
NX = 128
NY = 2048


def touch_ends(result, own_key, smallest, largest):
    dims = result.shape
    spot = [jax.random.randint(jax.random.fold_in(own_key, axis), (), 0, dims[axis]) for axis in range(len(dims))]
    result = result.at[tuple(spot)].set(smallest)
    longest = dims.index(max(dims))
    spot[longest] = (spot[longest] + 1) % dims[longest]
    return result.at[tuple(spot)].set(largest)


def levels(stream_key, dims, pieces, least, high):
    def one(axis_at, blocks):
        steps = jax.random.uniform(jax.random.fold_in(jax.random.fold_in(stream_key, 6), axis_at), (blocks,), jnp.float32, least / len(pieces), high / len(pieces))
        return jnp.repeat(jnp.exp(steps), dims[axis_at] // blocks).reshape((-1,) + (1,) * (len(dims) - axis_at - 1))

    level = one(*pieces[0])
    for cut in pieces[1:]:
        level = level * one(*cut)
    return level


def gaussian(rng, extent, width, limit, shards=(), kind=jnp.bfloat16):
    values = jax.random.normal(rng, extent, jnp.float32) * width
    if len(shards) > 0:
        values = levels(rng, extent, shards, -0.22, 0.18) * values
    return jnp.clip(values, min=-limit, max=limit).astype(kind)


def setup_inputs(seed: int = 0) -> dict:
    key_of = jax.random.split(jax.random.key(seed), 6)
    mask_levels = touch_ends(jax.random.randint(key_of[0], (NX, NY), 0, 4), jax.random.fold_in(key_of[0], 1), 0, 3).astype(jnp.int32)
    level_offset = gaussian(key_of[1], (NX, NY), 1.0, 6.0, ((0, 4), (1, 4)), jnp.float32)
    target_bits = touch_ends((jax.random.randint(key_of[2], (NX, NY), 0, 2) < 1).astype(jnp.int32), jax.random.fold_in(key_of[2], 1), 0, 1)
    socs_kernels = gaussian(key_of[3], (2, K, TAPS, TAPS), 0.0112, 0.067871094, ((1, 2),))
    kernel_weights = jnp.clip(jnp.exp(math.log(1.0) - 2.3025851 * jax.random.uniform(key_of[4], (K,), jnp.float32) ** levels(key_of[4], (K,), ((0, 2),), -0.2, 0.2)), 0.1, 1.0)
    return dict(mask_levels=mask_levels, level_offset=level_offset, target_bits=target_bits, socs_kernels=socs_kernels, kernel_weights=kernel_weights)


steepness = 4.0
threshold = 1.0
loss_gain = 32.0


def correlate(field, kernel):
    margin = TAPS // 2
    output = lax.conv_general_dilated(field[None, None], kernel[None, None], (1, 1), ((margin, margin), (margin, margin)), precision=lax.Precision.HIGHEST)
    return output[0, 0]


def reference(mask_levels, level_offset, target_bits, socs_kernels, kernel_weights):
    mask_full = jax.nn.sigmoid(2.0 * (mask_levels.astype(jnp.float32) - 1.5) + level_offset)
    mask_bf = lax.optimization_barrier(mask_full.astype(jnp.bfloat16)).astype(jnp.float32)
    kernels_full = socs_kernels.astype(jnp.float32)
    pairs = (kernels_full[0], kernels_full[1], kernel_weights)

    def intensity_step(running, kernel_pair):
        real_part, imag_part, weight = kernel_pair
        fields_re = correlate(mask_bf, real_part)
        fields_im = correlate(mask_bf, imag_part)
        return running + weight * (fields_re * fields_re + fields_im * fields_im), None

    intensity, _ = lax.scan(intensity_step, jnp.zeros((NX, NY), jnp.float32), pairs)
    resist = jax.nn.sigmoid(steepness * (intensity - threshold))
    slope_term = loss_gain * steepness * (resist - target_bits.astype(jnp.float32)) * resist * (1.0 - resist)

    def gradient_step(running, kernel_pair):
        real_part, imag_part, weight = kernel_pair
        fields_re = correlate(mask_bf, real_part)
        fields_im = correlate(mask_bf, imag_part)
        charge_re = lax.optimization_barrier((2.0 * weight * slope_term * fields_re).astype(jnp.bfloat16)).astype(jnp.float32)
        charge_im = lax.optimization_barrier((2.0 * weight * slope_term * fields_im).astype(jnp.bfloat16)).astype(jnp.float32)
        running = running + correlate(charge_re, real_part[::-1, ::-1]) + correlate(charge_im, imag_part[::-1, ::-1])
        return running, None

    adjoint, _ = lax.scan(gradient_step, jnp.zeros((NX, NY), jnp.float32), pairs)
    return resist, adjoint * mask_full * (1.0 - mask_full)
```

```python
import functools

import jax
import jax.numpy as jnp
from jax import lax
from jax.experimental import pallas as pl
from jax.experimental.pallas import tpu as pltpu
from jax.sharding import PartitionSpec as P

MESH = pl.DeviceIdType.MESH
F32 = jnp.float32
BF = jnp.bfloat16
TAPS = 35
HALF = 17
BY = 16
SLOT = BY + TAPS - 1
TALL = 5
STEPS = 7
CHUNK = 64
PART = 128


def sigmoid(value):
    return 1.0 / (1.0 + jnp.exp(-value))


def lane_of(shape):
    return lax.broadcasted_iota(jnp.int32, shape, 1)


def split_dot(value, picks):
    high = value.astype(BF)
    low = (value - high.astype(F32)).astype(BF)
    return jnp.dot(high, picks, preferred_element_type=F32) + jnp.dot(
        low, picks, preferred_element_type=F32
    )


def kernel(R, C, KN, levels_ref, offset_ref, target_ref, kern_ref, weight_ref,
           resist_ref, grad_ref, full_s, send_s, center_s, edge_s, taps_s, own_s, kern_s, kernx_s,
           weight_s, weightx_s, fields_s, charge_s,
           toep_s, image_s, tgt_s, qa_s, qb_s, rcomp_s, acc_s, adj_s, outsend_s, outrecv_s,
           msend, mrecv, esend, erecv, ksend, krecv, wsend, wrecv, osend, orecv):
    TR, TC = levels_ref.shape
    NX = R * TR
    G = R * KN
    ST = TC // G
    HALF_K = weight_ref.shape[1]
    CH = 2 * HALF_K
    groups = -(-(ST + 2 * HALF) // BY)
    tiles = TC // 128
    lead = 128 - 2 * HALF
    r, c, k = (lax.axis_index(name) for name in ("row", "col", "kern"))
    me = k * R + r
    first = [i for i in range(G) if (ST * i + lead) // 128 == 0]
    last = [i for i in range(G) if (ST * i + lead) // 128 == tiles]

    barrier = pltpu.get_barrier_semaphore()
    for d in range(1, G):
        peer = lax.rem(me + d, G)
        pl.semaphore_signal(barrier, inc=1, device_id=(lax.rem(peer, R), c, peer // R),
                            device_id_type=MESH)
    waits = jnp.int32(G - 1)
    for needy, step in ((first, 1), (last, -1)):
        for i in needy:
            has = (c + step >= 0) & (c + step < C) & (k == i // R)
            gets = (c - step >= 0) & (c - step < C) & (me == i)

            @pl.when(has)
            def _():
                pl.semaphore_signal(barrier, inc=1, device_id=(i % R, c + step, i // R),
                                    device_id_type=MESH)

            @pl.when(gets)
            def _():
                for rr in range(R):
                    pl.semaphore_signal(barrier, inc=1, device_id=(rr, c - step, k),
                                        device_id_type=MESH)

            waits = waits + jnp.where(has, 1, 0) + jnp.where(gets, R, 0)

    full = sigmoid(2.0 * (levels_ref[...].astype(F32) - 1.5) + offset_ref[...])
    full_s[...] = full
    send_s[0] = full.astype(BF)
    send_s[1] = target_ref[...].astype(F32).astype(BF)
    weight_s[...] = jnp.zeros((8, 128), F32)
    weight_s[0:1, 0:HALF_K] = weight_ref[...]

    pl.semaphore_wait(barrier, waits)

    def window(i):
        tile = (ST * i + lead) // 128
        return pl.multiple_of((jnp.clip(tile, 1, tiles - 1) - 1) * 128, 128)

    other = (r, c, 1 - k)
    kcopy = pltpu.make_async_remote_copy(kern_s, kernx_s, ksend, krecv,
                                         device_id=other, device_id_type=MESH)
    wcopy = pltpu.make_async_remote_copy(weight_s, weightx_s, wsend, wrecv,
                                         device_id=other, device_id_type=MESH)
    mcopies = []
    for d in range(1, R):
        rr = lax.rem(r + d, R)
        copy = pltpu.make_async_remote_copy(
            send_s.at[:, :, pl.ds(window(k * R + rr), 256)], center_s.at[r],
            msend.at[d - 1], mrecv.at[r], device_id=(rr, c, k), device_id_type=MESH)
        copy.start()
        mcopies.append(copy)

    def edge_copy(i, step, n, sender_row):
        low = TC - 128 if step == 1 else 0
        return pltpu.make_async_remote_copy(
            send_s.at[:, :, pl.ds(low, 128)], edge_s.at[sender_row],
            esend.at[n], erecv.at[sender_row],
            device_id=(i % R, c + step, i // R), device_id_type=MESH)

    edges = [(i, 1) for i in first] + [(i, -1) for i in last]
    for n, (i, step) in enumerate(edges):
        @pl.when((c + step >= 0) & (c + step < C) & (k == i // R))
        def _():
            edge_copy(i, step, n, r).start()
    wcopy.start()

    WIDE = STEPS * 256
    taps_s[...] = jnp.zeros(taps_s.shape, F32)
    for part in range(2):
        for n in range(HALF_K):
            base = (part * HALF_K + n) * 40
            taps_s[base : base + TAPS, 0:TAPS] = kern_ref[part, n].astype(F32)
    for t in range(STEPS):
        low = jnp.zeros((CH, 128), F32)
        high = jnp.zeros((CH, 128), F32)
        for q in range(TALL):
            taps = taps_s[pl.ds(t * TALL + q, CH, stride=40), :]
            begin = q * SLOT
            moved = taps if begin == 0 else pltpu.roll(taps, begin % 128, 1)
            lane = lane_of((CH, 128))
            if begin + TAPS <= 128:
                low = low + moved
            elif begin >= 128:
                high = high + moved
            else:
                low = low + jnp.where(lane >= begin, moved, 0.0)
                high = high + jnp.where(lane < begin, moved, 0.0)
        own_s[:, t * 256 : t * 256 + 128] = low
        own_s[:, t * 256 + 128 : t * 256 + 256] = high
    kern_s[:, 0:WIDE] = own_s[0:16, :].astype(BF)
    kern_s[:, WIDE:] = jnp.concatenate(
        [own_s[16:24, : WIDE // 2], own_s[16:24, WIDE // 2 :]], axis=0).astype(BF)
    kcopy.start()

    center_s[r] = send_s[:, :, pl.ds(window(me), 256)]
    image_s[0 : HALF * 8, :] = jnp.zeros((HALF * 8, 128), F32)
    tail = image_s.shape[0] - (HALF + NX) * 8
    image_s[(HALF + NX) * 8 :, :] = jnp.zeros((tail, 128), F32)
    acc_s[...] = jnp.zeros(acc_s.shape, F32)

    def build(group, base):
        for o in range(BY):
            moved = base if o == 0 else pltpu.roll(base, o, 1)
            toep_s[group * 256 + o * 16 : group * 256 + o * 16 + 16, :] = moved.astype(BF)

    build(0, own_s[0:16, :])

    for d in range(1, R):
        rr = lax.rem(r + d, R)
        pltpu.make_async_remote_copy(
            send_s.at[:, :, pl.ds(0, 256)], center_s.at[rr], msend.at[d - 1], mrecv.at[rr],
            device_id=(rr, c, k), device_id_type=MESH).wait_recv()
    for n, (i, step) in enumerate(edges):
        @pl.when((c - step >= 0) & (c - step < C) & (me == i))
        def _():
            for rr in range(R):
                edge_copy(i, step, n, rr).wait_recv()

    start = ST * me + lead
    tile = start // 128
    off = start - tile * 128
    is_first, is_last = tile == 0, tile == tiles
    col0 = c * TC + me * ST - 2 * HALF
    column = lane_of((TR, 256)) + col0
    inside = (column >= 0) & (column < C * TC)
    for rr in range(R):
        for part in range(2):
            mid = center_s[rr, part].astype(F32)
            side = edge_s[rr, part].astype(F32)
            a0, a1 = mid[:, :128], mid[:, 128:]
            t0 = jnp.where(is_first, side, jnp.where(is_last, a1, a0))
            t1 = jnp.where(is_first, a0, jnp.where(is_last, side, a1))
            both = jnp.concatenate([t0, t1], axis=1)
            view = jnp.where(inside, pltpu.roll(both, 256 - off, 1), 0.0)
            for g in range(groups):
                shift = BY * g + (0 if part == 0 else HALF)
                moved = view if shift == 0 else pltpu.roll(view, 256 - shift, 1)
                if part == 0:
                    image_s[pl.ds((HALF + TR * rr) * 8 + g, TR, stride=8), :] = moved[:, :128]
                else:
                    tgt_s[pl.ds(TR * rr * 8 + g, TR, stride=8), :] = moved[:, :128]

    def pack(n, carry):
        base = pl.multiple_of(n * 128, 128)
        rows = image_s[pl.ds(base, 22 * 8), :]
        lane = lane_of((17 * 8, 128))

        def slot(s, by):
            moved = rows if by == 0 else pltpu.roll(rows, by, 1)
            return moved[s * 8 : (s + 17) * 8]

        two = slot(2, 2 * SLOT)
        low = jnp.where(lane < SLOT, slot(0, 0), jnp.where(lane < 2 * SLOT, slot(1, SLOT), two))
        high = jnp.where(
            lane < 3 * SLOT - 128, two,
            jnp.where(lane < 4 * SLOT - 128, slot(3, 3 * SLOT - 128),
                      jnp.where(lane < 5 * SLOT - 128, slot(4, 4 * SLOT - 128), 0.0)))
        value = jnp.concatenate([low, high], axis=1)
        qa_s[pl.ds(base, 128), :] = value[:128].astype(BF)
        qb_s[pl.ds(base, 128), :] = value[8:].astype(BF)
        return carry

    lax.fori_loop(0, (NX + 32) // 16, pack, 0)

    kcopy.wait_recv()
    wcopy.wait_recv()
    theirs = kernx_s[:, 0:WIDE].astype(F32)
    rest = kernx_s[:, WIDE:].astype(F32)
    build(1, jnp.concatenate([own_s[16:24, :], theirs[0:8]], axis=0))
    build(2, jnp.concatenate(
        [theirs[8:16], jnp.concatenate([rest[0:8], rest[8:16]], axis=1)], axis=0))

    lane8 = lane_of((8, 128))
    mine, other_w = weight_s[...], weightx_s[...]
    channel_w = (mine + pltpu.roll(mine, HALF_K, 1) + pltpu.roll(other_w, CH, 1)
                 + pltpu.roll(other_w, CH + HALF_K, 1))
    weights = []
    for group in range(3):
        piece = channel_w if group == 0 else pltpu.roll(channel_w, 128 - 16 * group, 1)
        piece = jnp.where(lane8 < 16, piece, 0.0)
        for by in (16, 32, 64):
            piece = piece + pltpu.roll(piece, by, 1)
        weights.append(jnp.concatenate([piece, piece], axis=1)[0:1])

    M = CHUNK * 8
    gather = (lax.broadcasted_iota(jnp.int32, (256, 128), 0) // 16
              == lax.broadcasted_iota(jnp.int32, (256, 128), 1)).astype(F32).astype(BF)
    spread = (lax.broadcasted_iota(jnp.int32, (128, 256), 0)
              == lax.broadcasted_iota(jnp.int32, (128, 256), 1) // 16).astype(F32).astype(BF)
    group_at = lax.rem(lax.broadcasted_iota(jnp.int32, (PART, 128), 0), 8)
    field_col = lane_of((PART, 128)) + BY * group_at + (col0 + HALF)
    live = ((lane_of((PART, 128)) < BY) & (group_at < groups)
            & (field_col >= 0) & (field_col < C * TC))

    def forward(n):
        row0 = n * M
        pieces = []
        for t in range(STEPS):
            source = qa_s if t % 2 == 0 else qb_s
            at = row0 + (TALL * t - t % 2) * 8
            pieces.append(source[at : at + M, :])
        patches = jnp.concatenate(pieces, axis=1)
        for group in range(3):
            fields_s[row0 : row0 + M, group * 256 : (group + 1) * 256] = lax.dot_general(
                patches, toep_s[group * 256 : (group + 1) * 256, :],
                (((1,), (1,)), ((), ())), preferred_element_type=F32)

    def middle(n):
        for at in range(n * M, (n + 1) * M, PART):
            rows = slice(at, at + PART)
            power = None
            for group in range(3):
                f = fields_s[rows, group * 256 : (group + 1) * 256]
                term = weights[group] * f * f
                power = term if power is None else power + term
            resist = sigmoid(4.0 * (split_dot(power, gather) - 1.0))
            slope = jnp.where(
                live, 128.0 * (resist - tgt_s[rows, :]) * resist * (1.0 - resist), 0.0)
            rcomp_s[rows, :] = jnp.where(live, resist, 0.0)
            wide = split_dot(slope, spread)
            for group in range(3):
                cols = slice(group * 256, (group + 1) * 256)
                charge_s[rows, cols] = (
                    2.0 * weights[group] * wide * fields_s[rows, cols]).astype(BF)

    def backward(n):
        for t in range(STEPS):
            at = n * M + TALL * t * 8
            acc_s[at : at + M, :] += jnp.dot(
                charge_s[n * M : (n + 1) * M, :], toep_s[:, t * 256 : (t + 1) * 256],
                preferred_element_type=F32)

    fold = 128 // ST
    piece_rows = TR // fold

    def send_out(part, source, margin):
        for rr in range(R):
            total = None
            for g in range(groups):
                value = source[pl.ds(TR * rr * 8 + g, TR, stride=8), :]
                by = (BY * g - margin) % 128
                value = value if by == 0 else pltpu.roll(value, by, 1)
                total = value if total is None else total + value
            lane = lane_of((piece_rows, 128))
            packed = total[0:piece_rows]
            for q in range(1, fold):
                moved = pltpu.roll(total[q * piece_rows : (q + 1) * piece_rows], q * ST, 1)
                packed = jnp.where(lane < q * ST, packed, moved)
            outsend_s[part, rr] = packed
        copies = []
        for d in range(1, G):
            peer = lax.rem(me + d, G)
            copy = pltpu.make_async_remote_copy(
                outsend_s.at[part, lax.rem(peer, R)], outrecv_s.at[part, me],
                osend.at[part, d - 1], orecv.at[part, me],
                device_id=(lax.rem(peer, R), c, peer // R), device_id_type=MESH)
            copy.start()
            copies.append(copy)
        outrecv_s[part, me] = outsend_s[part, r]
        return copies

    chunks = NX // CHUNK
    forward(0)
    for n in range(chunks):
        if n + 1 < chunks:
            forward(n + 1)
        middle(n)
        if n + 1 < chunks:
            backward(n)
    ocopies = send_out(0, rcomp_s, HALF)
    backward(chunks - 1)

    def unpack(n, carry):
        base = pl.multiple_of((n * 16 + HALF - 4) * 8, 8)
        low = acc_s[pl.ds(base, 20 * 8), 0:128]
        high = acc_s[pl.ds(base, 20 * 8), 128:256]
        lane = lane_of((128, 128))

        def slot(value, s, by):
            moved = value if by == 0 else pltpu.roll(value, by, 1)
            return moved[(4 - s) * 8 : (20 - s) * 8]

        two = jnp.where(lane < 128 - 2 * SLOT, slot(low, 2, 128 - 2 * SLOT),
                        slot(high, 2, 128 - 2 * SLOT))
        total = (slot(low, 0, 0) + slot(low, 1, 128 - SLOT) + two
                 + slot(high, 3, 256 - 3 * SLOT) + slot(high, 4, 256 - 4 * SLOT))
        adj_s[pl.ds(pl.multiple_of(n * 128, 128), 128), :] = jnp.where(lane < SLOT, total, 0.0)
        return carry

    lax.fori_loop(0, NX // 16, unpack, 0)

    ocopies += send_out(1, adj_s, 2 * HALF)

    def receive(part):
        for d in range(1, G):
            peer = lax.rem(me + d, G)
            pltpu.make_async_remote_copy(
                outsend_s.at[part, r], outrecv_s.at[part, peer], osend.at[part, d - 1],
                orecv.at[part, peer],
                device_id=(lax.rem(peer, R), c, peer // R), device_id_type=MESH).wait_recv()

    lane = lane_of((piece_rows, 128))
    for part in range(2):
        receive(part)
        for p in range(tiles):
            for q in range(fold):
                rows = slice(q * piece_rows, (q + 1) * piece_rows)
                cols = slice(p * 128, (p + 1) * 128)
                merged = None
                for m in range(fold):
                    value = outrecv_s[part, p * fold + m]
                    by = ((m - q) * ST) % 128
                    value = value if by == 0 else pltpu.roll(value, by, 1)
                    merged = value if m == 0 else jnp.where(lane < m * ST, merged, value)
                if part == 0:
                    resist_ref[rows, cols] = merged
                else:
                    mask = full_s[rows, cols]
                    grad_ref[rows, cols] = merged * mask * (1.0 - mask)

    for copy in mcopies + ocopies:
        copy.wait_send()
    kcopy.wait_send()
    wcopy.wait_send()
    for n, (i, step) in enumerate(edges):
        @pl.when((c + step >= 0) & (c + step < C) & (k == i // R))
        def _():
            edge_copy(i, step, n, r).wait_send()


def per_device(sizes, mask_levels, level_offset, target_bits, socs_kernels, kernel_weights):
    R, C, KN = sizes
    TR, TC = mask_levels.shape
    NX = R * TR
    G = R * KN
    local = socs_kernels.shape[1]
    fold = 128 * G // TC
    vmem = pl.BlockSpec(memory_space=pltpu.VMEM)
    ends = 2 * max(1, R)
    out = jax.ShapeDtypeStruct((TR, TC), F32)
    return pl.pallas_call(
        functools.partial(kernel, R, C, KN),
        out_shape=(out, out),
        in_specs=[vmem] * 5,
        out_specs=(vmem, vmem),
        scratch_shapes=[
            pltpu.VMEM((TR, TC), F32),
            pltpu.VMEM((2, TR, TC), BF),
            pltpu.VMEM((R, 2, TR, 256), BF),
            pltpu.VMEM((R, 2, TR, 128), BF),
            pltpu.VMEM((2 * local * 40, 128), F32),
            pltpu.VMEM((2 * local, STEPS * 256), F32),
            pltpu.VMEM((16, STEPS * 384), BF),
            pltpu.VMEM((16, STEPS * 384), BF),
            pltpu.VMEM((8, 128), F32),
            pltpu.VMEM((8, 128), F32),
            pltpu.VMEM((NX * 8, 768), F32),
            pltpu.VMEM((NX * 8, 768), BF),
            pltpu.VMEM((768, STEPS * 256), BF),
            pltpu.VMEM(((NX + 40) * 8, 128), F32),
            pltpu.VMEM((NX * 8, 128), F32),
            pltpu.VMEM(((NX + 32) * 8, 256), BF),
            pltpu.VMEM(((NX + 32) * 8, 256), BF),
            pltpu.VMEM((NX * 8, 128), F32),
            pltpu.VMEM(((NX + 40) * 8, 256), F32),
            pltpu.VMEM((NX * 8, 128), F32),
            pltpu.VMEM((2, R, TR // fold, 128), F32),
            pltpu.VMEM((2, G, TR // fold, 128), F32),
            pltpu.SemaphoreType.DMA((R,)),
            pltpu.SemaphoreType.DMA((R,)),
            pltpu.SemaphoreType.DMA((ends,)),
            pltpu.SemaphoreType.DMA((R,)),
            pltpu.SemaphoreType.DMA,
            pltpu.SemaphoreType.DMA,
            pltpu.SemaphoreType.DMA,
            pltpu.SemaphoreType.DMA,
            pltpu.SemaphoreType.DMA((2, G)),
            pltpu.SemaphoreType.DMA((2, G)),
        ],
        compiler_params=pltpu.CompilerParams(
            collective_id=0, has_side_effects=True, vmem_limit_bytes=48 * 1024 * 1024),
    )(mask_levels, level_offset, target_bits, socs_kernels, kernel_weights[None])


def solution(mesh):
    sizes = tuple(mesh.shape[name] for name in ("row", "col", "kern"))
    return jax.shard_map(
        functools.partial(per_device, sizes),
        mesh=mesh,
        in_specs=(
            P("row", "col"),
            P("row", "col"),
            P("row", "col"),
            P(None, "kern", None, None),
            P("kern"),
        ),
        out_specs=(P("row", "col"), P("row", "col")),
        check_vma=False,
    )
```

```python
import functools

import jax
import jax.numpy as jnp
from jax import lax
from jax.experimental import pallas as pl
from jax.experimental.pallas import tpu as pltpu
from jax.sharding import PartitionSpec as P

MESH = pl.DeviceIdType.MESH
F32 = jnp.float32
BF = jnp.bfloat16
TAPS = 35
HALF = 17
BY = 16
SLOT = BY + TAPS - 1
TALL = 5
STEPS = 7
CHUNK = 64
PART = 128


def sigmoid(value):
    return 1.0 / (1.0 + jnp.exp(-value))


def lane_of(shape):
    return lax.broadcasted_iota(jnp.int32, shape, 1)


def split_dot(value, picks):
    high = value.astype(BF)
    low = (value - high.astype(F32)).astype(BF)
    return jnp.dot(high, picks, preferred_element_type=F32) + jnp.dot(
        low, picks, preferred_element_type=F32
    )


def kernel(R, C, KN, levels_ref, offset_ref, target_ref, kern_ref, weight_ref,
           out_ref, full_s, send_s, center_s, edge_s, taps_s, own_s, kern_s, kernx_s,
           weight_s, weightx_s, fields_s, charge_s,
           toep_s, image_s, tgt_s, qa_s, qb_s, rcomp_s, acc_s, adj_s, outsend_s, outrecv_s,
           msend, mrecv, esend, erecv, ksend, krecv, wsend, wrecv, osend, orecv):
    TR, TC = levels_ref.shape
    NX = R * TR
    G = R * KN
    ST = TC // G
    HALF_K = weight_ref.shape[1]
    CH = 2 * HALF_K
    groups = -(-(ST + 2 * HALF) // BY)
    tiles = TC // 128
    lead = 128 - 2 * HALF
    r, c, k = (lax.axis_index(name) for name in ("row", "col", "kern"))
    me = k * R + r
    first = [i for i in range(G) if (ST * i + lead) // 128 == 0]
    last = [i for i in range(G) if (ST * i + lead) // 128 == tiles]

    barrier = pltpu.get_barrier_semaphore()
    for d in range(1, G):
        peer = lax.rem(me + d, G)
        pl.semaphore_signal(barrier, inc=1, device_id=(lax.rem(peer, R), c, peer // R),
                            device_id_type=MESH)
    waits = jnp.int32(G - 1)
    for needy, step in ((first, 1), (last, -1)):
        for i in needy:
            has = (c + step >= 0) & (c + step < C) & (k == i // R)
            gets = (c - step >= 0) & (c - step < C) & (me == i)

            @pl.when(has)
            def _():
                pl.semaphore_signal(barrier, inc=1, device_id=(i % R, c + step, i // R),
                                    device_id_type=MESH)

            @pl.when(gets)
            def _():
                for rr in range(R):
                    pl.semaphore_signal(barrier, inc=1, device_id=(rr, c - step, k),
                                        device_id_type=MESH)

            waits = waits + jnp.where(has, 1, 0) + jnp.where(gets, R, 0)

    full = sigmoid(2.0 * (levels_ref[...].astype(F32) - 1.5) + offset_ref[...])
    full_s[...] = full
    send_s[0] = full.astype(BF)
    send_s[1] = target_ref[...].astype(F32).astype(BF)
    weight_s[...] = jnp.zeros((8, 128), F32)
    weight_s[0:1, 0:HALF_K] = weight_ref[...]

    pl.semaphore_wait(barrier, waits)

    def window(i):
        tile = (ST * i + lead) // 128
        return pl.multiple_of((jnp.clip(tile, 1, tiles - 1) - 1) * 128, 128)

    other = (r, c, 1 - k)
    kcopy = pltpu.make_async_remote_copy(kern_s, kernx_s, ksend, krecv,
                                         device_id=other, device_id_type=MESH)
    wcopy = pltpu.make_async_remote_copy(weight_s, weightx_s, wsend, wrecv,
                                         device_id=other, device_id_type=MESH)
    mcopies = []
    for d in range(1, R):
        rr = lax.rem(r + d, R)
        copy = pltpu.make_async_remote_copy(
            send_s.at[:, :, pl.ds(window(k * R + rr), 256)], center_s.at[r],
            msend.at[d - 1], mrecv.at[r], device_id=(rr, c, k), device_id_type=MESH)
        copy.start()
        mcopies.append(copy)

    def edge_copy(i, step, n, sender_row):
        low = TC - 128 if step == 1 else 0
        return pltpu.make_async_remote_copy(
            send_s.at[:, :, pl.ds(low, 128)], edge_s.at[sender_row],
            esend.at[n], erecv.at[sender_row],
            device_id=(i % R, c + step, i // R), device_id_type=MESH)

    edges = [(i, 1) for i in first] + [(i, -1) for i in last]
    for n, (i, step) in enumerate(edges):
        @pl.when((c + step >= 0) & (c + step < C) & (k == i // R))
        def _():
            edge_copy(i, step, n, r).start()
    wcopy.start()

    WIDE = STEPS * 256
    taps_s[...] = jnp.zeros(taps_s.shape, F32)
    for part in range(2):
        for n in range(HALF_K):
            base = (part * HALF_K + n) * 40
            taps_s[base : base + TAPS, 0:TAPS] = kern_ref[part, n].astype(F32)
    for t in range(STEPS):
        low = jnp.zeros((CH, 128), F32)
        high = jnp.zeros((CH, 128), F32)
        for q in range(TALL):
            taps = taps_s[pl.ds(t * TALL + q, CH, stride=40), :]
            begin = q * SLOT
            moved = taps if begin == 0 else pltpu.roll(taps, begin % 128, 1)
            lane = lane_of((CH, 128))
            if begin + TAPS <= 128:
                low = low + moved
            elif begin >= 128:
                high = high + moved
            else:
                low = low + jnp.where(lane >= begin, moved, 0.0)
                high = high + jnp.where(lane < begin, moved, 0.0)
        own_s[:, t * 256 : t * 256 + 128] = low
        own_s[:, t * 256 + 128 : t * 256 + 256] = high
    kern_s[:, 0:WIDE] = own_s[0:16, :].astype(BF)
    kern_s[:, WIDE:] = jnp.concatenate(
        [own_s[16:24, : WIDE // 2], own_s[16:24, WIDE // 2 :]], axis=0).astype(BF)
    kcopy.start()

    center_s[r] = send_s[:, :, pl.ds(window(me), 256)]
    image_s[0 : HALF * 8, :] = jnp.zeros((HALF * 8, 128), F32)
    tail = image_s.shape[0] - (HALF + NX) * 8
    image_s[(HALF + NX) * 8 :, :] = jnp.zeros((tail, 128), F32)
    acc_s[...] = jnp.zeros(acc_s.shape, F32)

    def build(group, base):
        for o in range(BY):
            moved = base if o == 0 else pltpu.roll(base, o, 1)
            toep_s[group * 256 + o * 16 : group * 256 + o * 16 + 16, :] = moved

    build(0, own_s[0:16, :].astype(BF))

    for d in range(1, R):
        rr = lax.rem(r + d, R)
        pltpu.make_async_remote_copy(
            send_s.at[:, :, pl.ds(0, 256)], center_s.at[rr], msend.at[d - 1], mrecv.at[rr],
            device_id=(rr, c, k), device_id_type=MESH).wait_recv()
    for n, (i, step) in enumerate(edges):
        @pl.when((c - step >= 0) & (c - step < C) & (me == i))
        def _():
            for rr in range(R):
                edge_copy(i, step, n, rr).wait_recv()

    start = ST * me + lead
    tile = start // 128
    off = start - tile * 128
    is_first, is_last = tile == 0, tile == tiles
    col0 = c * TC + me * ST - 2 * HALF
    column = lane_of((TR, 256)) + col0
    inside = (column >= 0) & (column < C * TC)
    for rr in range(R):
        for part in range(2):
            mid = center_s[rr, part].astype(F32)
            side = edge_s[rr, part].astype(F32)
            a0, a1 = mid[:, :128], mid[:, 128:]
            t0 = jnp.where(is_first, side, jnp.where(is_last, a1, a0))
            t1 = jnp.where(is_first, a0, jnp.where(is_last, side, a1))
            both = jnp.concatenate([t0, t1], axis=1)
            view = jnp.where(inside, pltpu.roll(both, 256 - off, 1), 0.0)
            for g in range(groups):
                shift = BY * g + (0 if part == 0 else HALF)
                moved = view if shift == 0 else pltpu.roll(view, 256 - shift, 1)
                if part == 0:
                    image_s[pl.ds((HALF + TR * rr) * 8 + g, TR, stride=8), :] = moved[:, :128]
                else:
                    tgt_s[pl.ds(TR * rr * 8 + g, TR, stride=8), :] = moved[:, :128]

    def pack(n):
        base = n * 128
        rows = image_s[base : base + 22 * 8, :]
        lane = lane_of((17 * 8, 128))

        def slot(s, by):
            moved = rows if by == 0 else pltpu.roll(rows, by, 1)
            return moved[s * 8 : (s + 17) * 8]

        two = slot(2, 2 * SLOT)
        low = jnp.where(lane < SLOT, slot(0, 0), jnp.where(lane < 2 * SLOT, slot(1, SLOT), two))
        high = jnp.where(
            lane < 3 * SLOT - 128, two,
            jnp.where(lane < 4 * SLOT - 128, slot(3, 3 * SLOT - 128),
                      jnp.where(lane < 5 * SLOT - 128, slot(4, 4 * SLOT - 128), 0.0)))
        value = jnp.concatenate([low, high], axis=1)
        qa_s[base : base + 128, :] = value[:128].astype(BF)
        qb_s[base : base + 128, :] = value[8:].astype(BF)

    packs = (NX + 32) // 16
    ready = (CHUNK + 32) // 16
    for n in range(ready):
        pack(n)

    kcopy.wait_recv()
    wcopy.wait_recv()
    theirs = kernx_s[:, 0:WIDE].astype(F32)
    rest = kernx_s[:, WIDE:].astype(F32)
    mixed = jnp.concatenate([own_s[16:24, :], theirs[0:8]], axis=0).astype(BF)
    distant = jnp.concatenate(
        [theirs[8:16], jnp.concatenate([rest[0:8], rest[8:16]], axis=1)], axis=0).astype(BF)

    lane8 = lane_of((8, 128))
    mine, other_w = weight_s[...], weightx_s[...]
    channel_w = (mine + pltpu.roll(mine, HALF_K, 1) + pltpu.roll(other_w, CH, 1)
                 + pltpu.roll(other_w, CH + HALF_K, 1))
    weights = []
    for group in range(3):
        piece = channel_w if group == 0 else pltpu.roll(channel_w, 128 - 16 * group, 1)
        piece = jnp.where(lane8 < 16, piece, 0.0)
        for by in (16, 32, 64):
            piece = piece + pltpu.roll(piece, by, 1)
        weights.append(jnp.concatenate([piece, piece], axis=1)[0:1])

    M = CHUNK * 8
    gather = (lax.broadcasted_iota(jnp.int32, (256, 128), 0) // 16
              == lax.broadcasted_iota(jnp.int32, (256, 128), 1)).astype(F32).astype(BF)
    spread = (lax.broadcasted_iota(jnp.int32, (128, 256), 0)
              == lax.broadcasted_iota(jnp.int32, (128, 256), 1) // 16).astype(F32).astype(BF)
    group_at = lax.rem(lax.broadcasted_iota(jnp.int32, (PART, 128), 0), 8)
    field_col = lane_of((PART, 128)) + BY * group_at + (col0 + HALF)
    live = ((lane_of((PART, 128)) < BY) & (group_at < groups)
            & (field_col >= 0) & (field_col < C * TC))

    def forward(n, group):
        row0 = n * M
        pieces = []
        for t in range(STEPS):
            source = qa_s if t % 2 == 0 else qb_s
            at = row0 + (TALL * t - t % 2) * 8
            pieces.append(source[at : at + M, :])
        patches = jnp.concatenate(pieces, axis=1)
        fields_s[row0 : row0 + M, group * 256 : (group + 1) * 256] = lax.dot_general(
            patches, toep_s[group * 256 : (group + 1) * 256, :],
            (((1,), (1,)), ((), ())), preferred_element_type=F32)

    def middle(at):
        if True:
            rows = slice(at, at + PART)
            power = None
            for group in range(3):
                f = fields_s[rows, group * 256 : (group + 1) * 256]
                term = weights[group] * f * f
                power = term if power is None else power + term
            resist = sigmoid(4.0 * (split_dot(power, gather) - 1.0))
            slope = jnp.where(
                live, 128.0 * (resist - tgt_s[rows, :]) * resist * (1.0 - resist), 0.0)
            rcomp_s[rows, :] = jnp.where(live, resist, 0.0)
            wide = split_dot(slope, spread)
            for group in range(3):
                cols = slice(group * 256, (group + 1) * 256)
                charge_s[rows, cols] = (
                    2.0 * weights[group] * wide * fields_s[rows, cols]).astype(BF)

    def backward(n, t):
        at = n * M + TALL * t * 8
        acc_s[at : at + M, :] += jnp.dot(
            charge_s[n * M : (n + 1) * M, :], toep_s[:, t * 256 : (t + 1) * 256],
            preferred_element_type=F32)

    fold = 128 // ST
    piece_rows = TR // fold

    def send_out(part, source, margin):
        for rr in range(R):
            total = None
            for g in range(groups):
                value = source[pl.ds(TR * rr * 8 + g, TR, stride=8), :]
                by = (BY * g - margin) % 128
                value = value if by == 0 else pltpu.roll(value, by, 1)
                total = value if total is None else total + value
            lane = lane_of((piece_rows, 128))
            packed = total[0:piece_rows]
            for q in range(1, fold):
                moved = pltpu.roll(total[q * piece_rows : (q + 1) * piece_rows], q * ST, 1)
                packed = jnp.where(lane < q * ST, packed, moved)
            outsend_s[part, rr] = packed
        copies = []
        for d in range(1, G):
            peer = lax.rem(me + d, G)
            copy = pltpu.make_async_remote_copy(
                outsend_s.at[part, lax.rem(peer, R)], outrecv_s.at[part, me],
                osend.at[part, d - 1], orecv.at[part, me],
                device_id=(lax.rem(peer, R), c, peer // R), device_id_type=MESH)
            copy.start()
            copies.append(copy)
        outrecv_s[part, me] = outsend_s[part, r]
        return copies

    def unpack(n):
        base = (n * 16 + HALF - 4) * 8
        low = acc_s[base : base + 20 * 8, 0:128]
        high = acc_s[base : base + 20 * 8, 128:256]
        lane = lane_of((128, 128))

        def slot(value, s, by):
            moved = value if by == 0 else pltpu.roll(value, by, 1)
            return moved[(4 - s) * 8 : (20 - s) * 8]

        two = jnp.where(lane < 128 - 2 * SLOT, slot(low, 2, 128 - 2 * SLOT),
                        slot(high, 2, 128 - 2 * SLOT))
        total = (slot(low, 0, 0) + slot(low, 1, 128 - SLOT) + two
                 + slot(high, 3, 256 - 3 * SLOT) + slot(high, 4, 256 - 4 * SLOT))
        adj_s[n * 128 : (n + 1) * 128, :] = jnp.where(lane < SLOT, total, 0.0)

    def interleave(*lists):
        order = sorted((((i + 0.5) / len(steps), n, i) for n, steps in enumerate(lists)
                        for i in range(len(steps))))
        for _, n, i in order:
            lists[n][i]()

    chunks = NX // CHUNK
    call = functools.partial

    def forwards(n):
        return [call(forward, n, group) for group in range(3)]

    def middles(n):
        return [call(middle, at) for at in range(n * M, (n + 1) * M, PART)]

    def backwards(n):
        return [call(backward, n, t) for t in range(STEPS)]

    def unpacks(n):
        def done(m):
            return NX // 16 if m == chunks - 1 else max(0, ((m + 1) * CHUNK - HALF) // 16)
        low = done(n - 1) if n > 0 else 0
        return [call(unpack, i) for i in range(low, done(n))]

    forward(0, 0)
    build(1, mixed)
    forward(0, 1)
    build(2, distant)
    forward(0, 2)
    for n in range(ready, packs):
        pack(n)
    interleave(middles(0), *([forwards(1)] if chunks > 1 else []))
    for n in range(chunks - 1):
        more = forwards(n + 2) if n + 2 < chunks else []
        interleave(backwards(n) + more, middles(n + 1))
    ocopies = send_out(0, rcomp_s, HALF)
    spare = [step for n in range(chunks - 1) for step in unpacks(n)]
    interleave(backwards(chunks - 1), spare)
    for step in unpacks(chunks - 1):
        step()
    ocopies += send_out(1, adj_s, 2 * HALF)

    def receive(part):
        for d in range(1, G):
            peer = lax.rem(me + d, G)
            pltpu.make_async_remote_copy(
                outsend_s.at[part, r], outrecv_s.at[part, peer], osend.at[part, d - 1],
                orecv.at[part, peer],
                device_id=(lax.rem(peer, R), c, peer // R), device_id_type=MESH).wait_recv()

    lane = lane_of((piece_rows, 128))
    for part in range(2):
        receive(part)
        for p in range(tiles):
            for q in range(fold):
                rows = slice(q * piece_rows, (q + 1) * piece_rows)
                cols = slice(p * 128, (p + 1) * 128)
                merged = None
                for m in range(fold):
                    value = outrecv_s[part, p * fold + m]
                    by = ((m - q) * ST) % 128
                    value = value if by == 0 else pltpu.roll(value, by, 1)
                    merged = value if m == 0 else jnp.where(lane < m * ST, merged, value)
                if part == 0:
                    out_ref[0, rows, cols] = merged
                else:
                    mask = full_s[rows, cols]
                    out_ref[1, rows, cols] = merged * mask * (1.0 - mask)

    for copy in mcopies + ocopies:
        copy.wait_send()
    kcopy.wait_send()
    wcopy.wait_send()
    for n, (i, step) in enumerate(edges):
        @pl.when((c + step >= 0) & (c + step < C) & (k == i // R))
        def _():
            edge_copy(i, step, n, r).wait_send()


def per_device(sizes, mask_levels, level_offset, target_bits, socs_kernels, kernel_weights):
    R, C, KN = sizes
    TR, TC = mask_levels.shape
    NX = R * TR
    G = R * KN
    local = socs_kernels.shape[1]
    fold = 128 * G // TC
    vmem = pl.BlockSpec(memory_space=pltpu.VMEM)
    ends = 2 * max(1, R)
    out = jax.ShapeDtypeStruct((2, TR, TC), F32)
    both = pl.pallas_call(
        functools.partial(kernel, R, C, KN),
        out_shape=out,
        in_specs=[vmem] * 5,
        out_specs=vmem,
        scratch_shapes=[
            pltpu.VMEM((TR, TC), F32),
            pltpu.VMEM((2, TR, TC), BF),
            pltpu.VMEM((R, 2, TR, 256), BF),
            pltpu.VMEM((R, 2, TR, 128), BF),
            pltpu.VMEM((2 * local * 40, 128), F32),
            pltpu.VMEM((2 * local, STEPS * 256), F32),
            pltpu.VMEM((16, STEPS * 384), BF),
            pltpu.VMEM((16, STEPS * 384), BF),
            pltpu.VMEM((8, 128), F32),
            pltpu.VMEM((8, 128), F32),
            pltpu.VMEM((NX * 8, 768), F32),
            pltpu.VMEM((NX * 8, 768), BF),
            pltpu.VMEM((768, STEPS * 256), BF),
            pltpu.VMEM(((NX + 40) * 8, 128), F32),
            pltpu.VMEM((NX * 8, 128), F32),
            pltpu.VMEM(((NX + 32) * 8, 256), BF),
            pltpu.VMEM(((NX + 32) * 8, 256), BF),
            pltpu.VMEM((NX * 8, 128), F32),
            pltpu.VMEM(((NX + 40) * 8, 256), F32),
            pltpu.VMEM((NX * 8, 128), F32),
            pltpu.VMEM((2, R, TR // fold, 128), F32),
            pltpu.VMEM((2, G, TR // fold, 128), F32),
            pltpu.SemaphoreType.DMA((R,)),
            pltpu.SemaphoreType.DMA((R,)),
            pltpu.SemaphoreType.DMA((ends,)),
            pltpu.SemaphoreType.DMA((R,)),
            pltpu.SemaphoreType.DMA,
            pltpu.SemaphoreType.DMA,
            pltpu.SemaphoreType.DMA,
            pltpu.SemaphoreType.DMA,
            pltpu.SemaphoreType.DMA((2, G)),
            pltpu.SemaphoreType.DMA((2, G)),
        ],
        compiler_params=pltpu.CompilerParams(
            collective_id=0, has_side_effects=True, vmem_limit_bytes=48 * 1024 * 1024),
    )(mask_levels, level_offset, target_bits, socs_kernels, kernel_weights[None])
    return (both[0], both[1])


def solution(mesh):
    sizes = tuple(mesh.shape[name] for name in ("row", "col", "kern"))
    return jax.shard_map(
        functools.partial(per_device, sizes),
        mesh=mesh,
        in_specs=(
            P("row", "col"),
            P("row", "col"),
            P("row", "col"),
            P(None, "kern", None, None),
            P("kern"),
        ),
        out_specs=(P("row", "col"), P("row", "col")),
        check_vma=False,
    )
```

```python
import functools

import jax
import jax.numpy as jnp
from jax import lax
from jax.experimental import pallas as pl
from jax.experimental.pallas import tpu as pltpu
from jax.sharding import PartitionSpec as P

MESH = pl.DeviceIdType.MESH
F32 = jnp.float32
BF = jnp.bfloat16
TAPS = 35
HALF = 17
BY = 16
SLOT = BY + TAPS - 1
TALL = 5
STEPS = 7
CHUNK = 64
PART = 128


def sigmoid(value):
    return 1.0 / (1.0 + jnp.exp(-value))


def lane_of(shape):
    return lax.broadcasted_iota(jnp.int32, shape, 1)


def split_dot(value, picks):
    high = value.astype(BF)
    low = (value - high.astype(F32)).astype(BF)
    return jnp.dot(high, picks, preferred_element_type=F32) + jnp.dot(
        low, picks, preferred_element_type=F32
    )


def kernel(R, C, KN, levels_ref, offset_ref, target_ref, kern_ref, weight_ref,
           out_ref, full_s, send_s, center_s, edge_s, taps_s, own_s, kern_s, kernx_s,
           weight_s, weightx_s, fields_s, charge_s,
           toep_s, image_s, tgt_s, qa_s, qb_s, rcomp_s, acc_s, adj_s, outsend_s, outrecv_s,
           msend, mrecv, esend, erecv, ksend, krecv, wsend, wrecv, osend, orecv):
    TR, TC = levels_ref.shape
    NX = R * TR
    G = R * KN
    ST = TC // G
    HALF_K = weight_ref.shape[1]
    CH = 2 * HALF_K
    groups = -(-(ST + 2 * HALF) // BY)
    tiles = TC // 128
    lead = 128 - 2 * HALF
    r, c, k = (lax.axis_index(name) for name in ("row", "col", "kern"))
    me = k * R + r
    first = [i for i in range(G) if (ST * i + lead) // 128 == 0]
    last = [i for i in range(G) if (ST * i + lead) // 128 == tiles]

    barrier = pltpu.get_barrier_semaphore()
    for d in range(1, G):
        peer = lax.rem(me + d, G)
        pl.semaphore_signal(barrier, inc=1, device_id=(lax.rem(peer, R), c, peer // R),
                            device_id_type=MESH)
    waits = jnp.int32(G - 1)
    for needy, step in ((first, 1), (last, -1)):
        for i in needy:
            has = (c + step >= 0) & (c + step < C) & (k == i // R)
            gets = (c - step >= 0) & (c - step < C) & (me == i)

            @pl.when(has)
            def _():
                pl.semaphore_signal(barrier, inc=1, device_id=(i % R, c + step, i // R),
                                    device_id_type=MESH)

            @pl.when(gets)
            def _():
                for rr in range(R):
                    pl.semaphore_signal(barrier, inc=1, device_id=(rr, c - step, k),
                                        device_id_type=MESH)

            waits = waits + jnp.where(has, 1, 0) + jnp.where(gets, R, 0)

    full = sigmoid(2.0 * (levels_ref[...].astype(F32) - 1.5) + offset_ref[...])
    full_s[...] = full
    send_s[0] = full.astype(BF)
    send_s[1] = target_ref[...].astype(F32).astype(BF)
    weight_s[...] = jnp.zeros((8, 128), F32)
    weight_s[0:1, 0:HALF_K] = weight_ref[...]

    WIDE = STEPS * 256
    taps_s[...] = jnp.zeros(taps_s.shape, F32)
    for part in range(2):
        for n in range(HALF_K):
            base = (part * HALF_K + n) * 40
            taps_s[base : base + TAPS, 0:TAPS] = kern_ref[part, n].astype(F32)
    for t in range(STEPS):
        low = jnp.zeros((CH, 128), F32)
        high = jnp.zeros((CH, 128), F32)
        for q in range(TALL):
            taps = taps_s[pl.ds(t * TALL + q, CH, stride=40), :]
            begin = q * SLOT
            moved = taps if begin == 0 else pltpu.roll(taps, begin % 128, 1)
            lane = lane_of((CH, 128))
            if begin + TAPS <= 128:
                low = low + moved
            elif begin >= 128:
                high = high + moved
            else:
                low = low + jnp.where(lane >= begin, moved, 0.0)
                high = high + jnp.where(lane < begin, moved, 0.0)
        own_s[:, t * 256 : t * 256 + 128] = low
        own_s[:, t * 256 + 128 : t * 256 + 256] = high
    kern_s[:, 0:WIDE] = own_s[0:16, :].astype(BF)
    kern_s[:, WIDE:] = jnp.concatenate(
        [own_s[16:24, : WIDE // 2], own_s[16:24, WIDE // 2 :]], axis=0).astype(BF)

    pl.semaphore_wait(barrier, waits)

    def window(i):
        tile = (ST * i + lead) // 128
        return pl.multiple_of((jnp.clip(tile, 1, tiles - 1) - 1) * 128, 128)

    other = (r, c, 1 - k)
    kcopy = pltpu.make_async_remote_copy(kern_s, kernx_s, ksend, krecv,
                                         device_id=other, device_id_type=MESH)
    wcopy = pltpu.make_async_remote_copy(weight_s, weightx_s, wsend, wrecv,
                                         device_id=other, device_id_type=MESH)
    mcopies = []
    for d in range(1, R):
        rr = lax.rem(r + d, R)
        copy = pltpu.make_async_remote_copy(
            send_s.at[:, :, pl.ds(window(k * R + rr), 256)], center_s.at[r],
            msend.at[d - 1], mrecv.at[r], device_id=(rr, c, k), device_id_type=MESH)
        copy.start()
        mcopies.append(copy)

    def edge_copy(i, step, n, sender_row):
        low = TC - 128 if step == 1 else 0
        return pltpu.make_async_remote_copy(
            send_s.at[:, :, pl.ds(low, 128)], edge_s.at[sender_row],
            esend.at[n], erecv.at[sender_row],
            device_id=(i % R, c + step, i // R), device_id_type=MESH)

    edges = [(i, 1) for i in first] + [(i, -1) for i in last]
    for n, (i, step) in enumerate(edges):
        @pl.when((c + step >= 0) & (c + step < C) & (k == i // R))
        def _():
            edge_copy(i, step, n, r).start()
    wcopy.start()
    kcopy.start()

    center_s[r] = send_s[:, :, pl.ds(window(me), 256)]
    image_s[0 : HALF * 8, :] = jnp.zeros((HALF * 8, 128), F32)
    tail = image_s.shape[0] - (HALF + NX) * 8
    image_s[(HALF + NX) * 8 :, :] = jnp.zeros((tail, 128), F32)
    acc_s[...] = jnp.zeros(acc_s.shape, F32)

    def build(group, base):
        for o in range(BY):
            moved = base if o == 0 else pltpu.roll(base, o, 1)
            toep_s[group * 256 + o * 16 : group * 256 + o * 16 + 16, :] = moved

    build(0, own_s[0:16, :].astype(BF))

    for d in range(1, R):
        rr = lax.rem(r + d, R)
        pltpu.make_async_remote_copy(
            send_s.at[:, :, pl.ds(0, 256)], center_s.at[rr], msend.at[d - 1], mrecv.at[rr],
            device_id=(rr, c, k), device_id_type=MESH).wait_recv()
    for n, (i, step) in enumerate(edges):
        @pl.when((c - step >= 0) & (c - step < C) & (me == i))
        def _():
            for rr in range(R):
                edge_copy(i, step, n, rr).wait_recv()

    start = ST * me + lead
    tile = start // 128
    off = start - tile * 128
    is_first, is_last = tile == 0, tile == tiles
    col0 = c * TC + me * ST - 2 * HALF
    column = lane_of((TR, 256)) + col0
    inside = (column >= 0) & (column < C * TC)
    for rr in range(R):
        for part in range(2):
            mid = center_s[rr, part].astype(F32)
            side = edge_s[rr, part].astype(F32)
            a0, a1 = mid[:, :128], mid[:, 128:]
            t0 = jnp.where(is_first, side, jnp.where(is_last, a1, a0))
            t1 = jnp.where(is_first, a0, jnp.where(is_last, side, a1))
            both = jnp.concatenate([t0, t1], axis=1)
            view = jnp.where(inside, pltpu.roll(both, 256 - off, 1), 0.0)
            for g in range(groups):
                shift = BY * g + (0 if part == 0 else HALF)
                moved = view if shift == 0 else pltpu.roll(view, 256 - shift, 1)
                if part == 0:
                    image_s[pl.ds((HALF + TR * rr) * 8 + g, TR, stride=8), :] = moved[:, :128]
                else:
                    tgt_s[pl.ds(TR * rr * 8 + g, TR, stride=8), :] = moved[:, :128]

    def pack(n):
        base = n * 128
        rows = image_s[base : base + 22 * 8, :]
        lane = lane_of((17 * 8, 128))

        def slot(s, by):
            moved = rows if by == 0 else pltpu.roll(rows, by, 1)
            return moved[s * 8 : (s + 17) * 8]

        two = slot(2, 2 * SLOT)
        low = jnp.where(lane < SLOT, slot(0, 0), jnp.where(lane < 2 * SLOT, slot(1, SLOT), two))
        high = jnp.where(
            lane < 3 * SLOT - 128, two,
            jnp.where(lane < 4 * SLOT - 128, slot(3, 3 * SLOT - 128),
                      jnp.where(lane < 5 * SLOT - 128, slot(4, 4 * SLOT - 128), 0.0)))
        value = jnp.concatenate([low, high], axis=1)
        qa_s[base : base + 128, :] = value[:128].astype(BF)
        qb_s[base : base + 128, :] = value[8:].astype(BF)

    packs = (NX + 32) // 16
    ready = (CHUNK + 32) // 16
    for n in range(ready):
        pack(n)

    kcopy.wait_recv()
    wcopy.wait_recv()
    theirs = kernx_s[:, 0:WIDE].astype(F32)
    rest = kernx_s[:, WIDE:].astype(F32)
    mixed = jnp.concatenate([own_s[16:24, :], theirs[0:8]], axis=0).astype(BF)
    distant = jnp.concatenate(
        [theirs[8:16], jnp.concatenate([rest[0:8], rest[8:16]], axis=1)], axis=0).astype(BF)

    lane8 = lane_of((8, 128))
    mine, other_w = weight_s[...], weightx_s[...]
    channel_w = (mine + pltpu.roll(mine, HALF_K, 1) + pltpu.roll(other_w, CH, 1)
                 + pltpu.roll(other_w, CH + HALF_K, 1))
    weights = []
    for group in range(3):
        piece = channel_w if group == 0 else pltpu.roll(channel_w, 128 - 16 * group, 1)
        piece = jnp.where(lane8 < 16, piece, 0.0)
        for by in (16, 32, 64):
            piece = piece + pltpu.roll(piece, by, 1)
        weights.append(jnp.concatenate([piece, piece], axis=1)[0:1])

    M = CHUNK * 8
    gather = (lax.broadcasted_iota(jnp.int32, (256, 128), 0) // 16
              == lax.broadcasted_iota(jnp.int32, (256, 128), 1)).astype(F32).astype(BF)
    spread = (lax.broadcasted_iota(jnp.int32, (128, 256), 0)
              == lax.broadcasted_iota(jnp.int32, (128, 256), 1) // 16).astype(F32).astype(BF)
    group_at = lax.rem(lax.broadcasted_iota(jnp.int32, (PART, 128), 0), 8)
    field_col = lane_of((PART, 128)) + BY * group_at + (col0 + HALF)
    live = ((lane_of((PART, 128)) < BY) & (group_at < groups)
            & (field_col >= 0) & (field_col < C * TC))

    def forward(n, group):
        row0 = n * M
        pieces = []
        for t in range(STEPS):
            source = qa_s if t % 2 == 0 else qb_s
            at = row0 + (TALL * t - t % 2) * 8
            pieces.append(source[at : at + M, :])
        patches = jnp.concatenate(pieces, axis=1)
        fields_s[row0 : row0 + M, group * 256 : (group + 1) * 256] = lax.dot_general(
            patches, toep_s[group * 256 : (group + 1) * 256, :],
            (((1,), (1,)), ((), ())), preferred_element_type=F32)

    def middle(at):
        if True:
            rows = slice(at, at + PART)
            power = None
            for group in range(3):
                f = fields_s[rows, group * 256 : (group + 1) * 256]
                term = weights[group] * f * f
                power = term if power is None else power + term
            resist = sigmoid(4.0 * (split_dot(power, gather) - 1.0))
            slope = jnp.where(
                live, 128.0 * (resist - tgt_s[rows, :]) * resist * (1.0 - resist), 0.0)
            rcomp_s[rows, :] = jnp.where(live, resist, 0.0)
            wide = split_dot(slope, spread)
            for group in range(3):
                cols = slice(group * 256, (group + 1) * 256)
                charge_s[rows, cols] = (
                    2.0 * weights[group] * wide * fields_s[rows, cols]).astype(BF)

    def backward(n, t):
        at = n * M + TALL * t * 8
        acc_s[at : at + M, :] += jnp.dot(
            charge_s[n * M : (n + 1) * M, :], toep_s[:, t * 256 : (t + 1) * 256],
            preferred_element_type=F32)

    fold = 128 // ST
    piece_rows = TR // fold

    def send_out(part, source, margin):
        for rr in range(R):
            total = None
            for g in range(groups):
                value = source[pl.ds(TR * rr * 8 + g, TR, stride=8), :]
                by = (BY * g - margin) % 128
                value = value if by == 0 else pltpu.roll(value, by, 1)
                total = value if total is None else total + value
            lane = lane_of((piece_rows, 128))
            packed = total[0:piece_rows]
            for q in range(1, fold):
                moved = pltpu.roll(total[q * piece_rows : (q + 1) * piece_rows], q * ST, 1)
                packed = jnp.where(lane < q * ST, packed, moved)
            outsend_s[part, rr] = packed
        copies = []
        for d in range(1, G):
            peer = lax.rem(me + d, G)
            copy = pltpu.make_async_remote_copy(
                outsend_s.at[part, lax.rem(peer, R)], outrecv_s.at[part, me],
                osend.at[part, d - 1], orecv.at[part, me],
                device_id=(lax.rem(peer, R), c, peer // R), device_id_type=MESH)
            copy.start()
            copies.append(copy)
        outrecv_s[part, me] = outsend_s[part, r]
        return copies

    def unpack(n):
        base = (n * 16 + HALF - 4) * 8
        low = acc_s[base : base + 20 * 8, 0:128]
        high = acc_s[base : base + 20 * 8, 128:256]
        lane = lane_of((128, 128))

        def slot(value, s, by):
            moved = value if by == 0 else pltpu.roll(value, by, 1)
            return moved[(4 - s) * 8 : (20 - s) * 8]

        two = jnp.where(lane < 128 - 2 * SLOT, slot(low, 2, 128 - 2 * SLOT),
                        slot(high, 2, 128 - 2 * SLOT))
        total = (slot(low, 0, 0) + slot(low, 1, 128 - SLOT) + two
                 + slot(high, 3, 256 - 3 * SLOT) + slot(high, 4, 256 - 4 * SLOT))
        adj_s[n * 128 : (n + 1) * 128, :] = jnp.where(lane < SLOT, total, 0.0)

    def interleave(*lists):
        order = sorted((((i + 0.5) / len(steps), n, i) for n, steps in enumerate(lists)
                        for i in range(len(steps))))
        for _, n, i in order:
            lists[n][i]()

    chunks = NX // CHUNK
    call = functools.partial

    def forwards(n):
        return [call(forward, n, group) for group in range(3)]

    def middles(n):
        return [call(middle, at) for at in range(n * M, (n + 1) * M, PART)]

    def backwards(n):
        return [call(backward, n, t) for t in range(STEPS)]

    def unpacks(n):
        def done(m):
            return NX // 16 if m == chunks - 1 else max(0, ((m + 1) * CHUNK - HALF) // 16)
        low = done(n - 1) if n > 0 else 0
        return [call(unpack, i) for i in range(low, done(n))]

    forward(0, 0)
    build(1, mixed)
    forward(0, 1)
    build(2, distant)
    forward(0, 2)
    for n in range(ready, packs):
        pack(n)
    interleave(middles(0), *([forwards(1)] if chunks > 1 else []))
    for n in range(chunks - 1):
        more = forwards(n + 2) if n + 2 < chunks else []
        interleave(backwards(n) + more, middles(n + 1))
    ocopies = send_out(0, rcomp_s, HALF)
    spare = [step for n in range(chunks - 1) for step in unpacks(n)]
    interleave(backwards(chunks - 1), spare)
    for step in unpacks(chunks - 1):
        step()
    ocopies += send_out(1, adj_s, 2 * HALF)

    def receive(part):
        for d in range(1, G):
            peer = lax.rem(me + d, G)
            pltpu.make_async_remote_copy(
                outsend_s.at[part, r], outrecv_s.at[part, peer], osend.at[part, d - 1],
                orecv.at[part, peer],
                device_id=(lax.rem(peer, R), c, peer // R), device_id_type=MESH).wait_recv()

    lane = lane_of((piece_rows, 128))
    for part in range(2):
        receive(part)
        for p in range(tiles):
            for q in range(fold):
                rows = slice(q * piece_rows, (q + 1) * piece_rows)
                cols = slice(p * 128, (p + 1) * 128)
                merged = None
                for m in range(fold):
                    value = outrecv_s[part, p * fold + m]
                    by = ((m - q) * ST) % 128
                    value = value if by == 0 else pltpu.roll(value, by, 1)
                    merged = value if m == 0 else jnp.where(lane < m * ST, merged, value)
                if part == 0:
                    out_ref[0, rows, cols] = merged
                else:
                    mask = full_s[rows, cols]
                    out_ref[1, rows, cols] = merged * mask * (1.0 - mask)

    for copy in mcopies + ocopies:
        copy.wait_send()
    kcopy.wait_send()
    wcopy.wait_send()
    for n, (i, step) in enumerate(edges):
        @pl.when((c + step >= 0) & (c + step < C) & (k == i // R))
        def _():
            edge_copy(i, step, n, r).wait_send()


def per_device(sizes, mask_levels, level_offset, target_bits, socs_kernels, kernel_weights):
    R, C, KN = sizes
    TR, TC = mask_levels.shape
    NX = R * TR
    G = R * KN
    local = socs_kernels.shape[1]
    fold = 128 * G // TC
    vmem = pl.BlockSpec(memory_space=pltpu.VMEM)
    ends = 2 * max(1, R)
    out = jax.ShapeDtypeStruct((2, TR, TC), F32)
    both = pl.pallas_call(
        functools.partial(kernel, R, C, KN),
        out_shape=out,
        in_specs=[vmem] * 5,
        out_specs=vmem,
        scratch_shapes=[
            pltpu.VMEM((TR, TC), F32),
            pltpu.VMEM((2, TR, TC), BF),
            pltpu.VMEM((R, 2, TR, 256), BF),
            pltpu.VMEM((R, 2, TR, 128), BF),
            pltpu.VMEM((2 * local * 40, 128), F32),
            pltpu.VMEM((2 * local, STEPS * 256), F32),
            pltpu.VMEM((16, STEPS * 384), BF),
            pltpu.VMEM((16, STEPS * 384), BF),
            pltpu.VMEM((8, 128), F32),
            pltpu.VMEM((8, 128), F32),
            pltpu.VMEM((NX * 8, 768), F32),
            pltpu.VMEM((NX * 8, 768), BF),
            pltpu.VMEM((768, STEPS * 256), BF),
            pltpu.VMEM(((NX + 40) * 8, 128), F32),
            pltpu.VMEM((NX * 8, 128), F32),
            pltpu.VMEM(((NX + 32) * 8, 256), BF),
            pltpu.VMEM(((NX + 32) * 8, 256), BF),
            pltpu.VMEM((NX * 8, 128), F32),
            pltpu.VMEM(((NX + 40) * 8, 256), F32),
            pltpu.VMEM((NX * 8, 128), F32),
            pltpu.VMEM((2, R, TR // fold, 128), F32),
            pltpu.VMEM((2, G, TR // fold, 128), F32),
            pltpu.SemaphoreType.DMA((R,)),
            pltpu.SemaphoreType.DMA((R,)),
            pltpu.SemaphoreType.DMA((ends,)),
            pltpu.SemaphoreType.DMA((R,)),
            pltpu.SemaphoreType.DMA,
            pltpu.SemaphoreType.DMA,
            pltpu.SemaphoreType.DMA,
            pltpu.SemaphoreType.DMA,
            pltpu.SemaphoreType.DMA((2, G)),
            pltpu.SemaphoreType.DMA((2, G)),
        ],
        compiler_params=pltpu.CompilerParams(
            collective_id=0, has_side_effects=True, vmem_limit_bytes=48 * 1024 * 1024),
    )(mask_levels, level_offset, target_bits, socs_kernels, kernel_weights[None])
    return (both[0], both[1])


def solution(mesh):
    sizes = tuple(mesh.shape[name] for name in ("row", "col", "kern"))
    return jax.shard_map(
        functools.partial(per_device, sizes),
        mesh=mesh,
        in_specs=(
            P("row", "col"),
            P("row", "col"),
            P("row", "col"),
            P(None, "kern", None, None),
            P("kern"),
        ),
        out_specs=(P("row", "col"), P("row", "col")),
        check_vma=False,
    )
```
